32 devices in a mesh: seq: 16 (over z, x, core), tp: 2 (over y).
Axes of the slice: x: 2, y: 2, z: 4, core: 2. Of those that a mesh axis runs over, the one named last changes fastest.
Arguments:
- queries: bfloat16 [4096, 3072], P(('seq', 'tp')), may hold values from -42 to 42
- keys: bfloat16 [4096, 3072], P(('seq', 'tp')), may hold values from -6 to 6
- values: bfloat16 [4096, 3072], P(('seq', 'tp')), may hold values from -6 to 6
- pool_keys: bfloat16 [16, 128, 3072], P('seq', None, 'tp'), may hold values from -6 to 6
- pool_values: bfloat16 [16, 128, 3072], P('seq', None, 'tp'), may hold values from -6 to 6
- page_table: int32 [16], replicated, may hold values from 0 to 15, each once
- lengths: int32 [32], replicated, may hold values from 1 to 256, 4096 in all
- group_of: int32 [32], replicated, may hold values from 0 to 1
Outputs:
- context: bfloat16 [4096, 3072], P(('seq', 'tp'))
- new_keys: bfloat16 [4096, 3072], P('seq', 'tp')
- new_values: bfloat16 [4096, 3072], P('seq', 'tp')
The draws below stay inside these ranges and needn't reach their ends.
Inputs may be any that keep to these rules, and one draw needn't show every extreme that they name: `page_table`: each of the 16 slots appears once; entries g * 8 to (g + 1) * 8 - 1 are group g's pages; slot s lies on index s of seq. The lengths sum to 4096; each request's suffix tokens follow those of the requests before it.
All inputs are finite; a program needn't handle non-finite values.
Results may differ from the reference program's by a relative error of at most 0.0055.
Values may be sent and summed in bfloat16 or wider, within the bound.
No kernel may reach another device: no remote copies, remote signals or barrier semaphores. Data moves between devices by JAX's collectives and lax.ppermute only.
A program may use at most 64 MiB of HBM per device.

```python
import math
import jax
import jax.numpy as jnp
import numpy as np
from jax import lax

H = 32
HD = 96
ROT = 24
PAGE = 128
SUF_MAX = 256
TOK_DEV = 256
C = 3072
TOKENS = 4096
REQS = 32
SLOTS = 16
PAGES_GROUP = 8
PREFIX = 1024


def draw_queries(key, part):
    base_key = jax.random.fold_in(key, 21)
    entries = jnp.clip(2.5 * jax.random.normal(base_key, (TOKENS, C), jnp.float32), -7.5, 7.5)
    return entries.astype(jnp.bfloat16)


def draw_pool_keys(key, part):
    base_key = jax.random.fold_in(key, 31)
    entries = jnp.clip(jax.random.normal(base_key, (SLOTS * PAGE, C), jnp.float32), -6.0, 6.0)
    return entries.reshape(SLOTS, PAGE, C).astype(jnp.bfloat16)


def set_ends(values, key, smallest, largest):
    longest = values.shape.index(max(values.shape))
    spots = []
    for shift in (0, 1):
        where = [jax.random.randint(jax.random.fold_in(key, axis), (), 0, length) for axis, length in enumerate(values.shape)]
        where[longest] = (where[longest] + shift) % values.shape[longest]
        spots.append(tuple(where))
    return values.at[spots[0]].set(smallest).at[spots[1]].set(largest)


def steps_of(rng, dims, pieces, smallest, high):
    level = 1.0
    for dim, parts in pieces:
        steps = jax.random.uniform(jax.random.fold_in(jax.random.fold_in(rng, 6), dim), (parts,), jnp.float32, smallest / len(pieces), high / len(pieces))
        level = level * jnp.repeat(jnp.exp(steps), dims[dim] // parts).reshape((-1,) + (1,) * (len(dims) - 1 - dim))
    return level


def split_up(amount, total, reach, lean):
    weights = [(1 << 20) // math.isqrt(grade ** lean) + 1 for grade in range(2, amount + 1)]
    rest, given = total - reach - (amount - 1), [1] * (amount - 1)
    while rest > 0:
        free = [i for i in range(amount - 1) if given[i] < reach]
        pool, budget = sum([weights[i] for i in free]), rest
        for i in free:
            more = min(reach - given[i], max(1, budget * weights[i] // pool), rest)
            given[i] = given[i] + more
            rest = rest - more
    return np.array([reach] + given)


def uneven(stream_key, number_of, total, limit, slope):
    if number_of == 2:
        one = jax.random.randint(stream_key, (), max(1, total - limit), min(limit, total - 1) + 1)
        return jnp.stack([one, total - one])
    sizes = jnp.asarray(split_up(number_of, total, limit, slope), jnp.int32)
    couples = (number_of - 1) // 2
    source_of, receiver = sizes[1:1 + 2 * couples:2], sizes[2:2 + 2 * couples:2]
    room = jnp.minimum(source_of - 1, limit - receiver)
    moved = jax.random.randint(jax.random.fold_in(stream_key, 1), (couples,), 0, 1 << 20) % (room + 1)
    sizes = sizes.at[1:1 + 2 * couples:2].set(source_of - moved).at[2:2 + 2 * couples:2].set(receiver + moved)
    return sizes[jax.random.permutation(jax.random.fold_in(stream_key, 2), number_of)]


def gaussian(rng, shape, scale, bound, split=(), held_as=jnp.bfloat16):
    gain = steps_of(rng, shape, split, -0.22, 0.18) if split else 1.0
    values = jax.random.normal(rng, shape, jnp.float32) * scale * gain
    return jnp.minimum(jnp.maximum(values, -bound), bound).astype(held_as)


def setup_inputs(seed: int = 0) -> dict:
    key_list = jax.random.split(jax.random.key(seed), 9)
    return {
        "queries": draw_queries(jax.random.fold_in(key_list[8], 71), 0),
        "keys": gaussian(key_list[1], (TOKENS, C), 1.0, 6.0, ((0, 32),)),
        "values": gaussian(key_list[2], (TOKENS, C), 1.0, 6.0, ((0, 32),)),
        "pool_keys": draw_pool_keys(jax.random.fold_in(key_list[8], 71), 0),
        "pool_values": gaussian(key_list[4], (SLOTS, PAGE, C), 1.0, 6.0, ((0, 16), (2, 2))),
        "page_table": jax.random.permutation(key_list[5], SLOTS).astype(jnp.int32),
        "lengths": uneven(key_list[6], REQS, TOKENS, SUF_MAX, 2).astype(jnp.int32),
        "group_of": set_ends(jax.random.randint(key_list[7], (REQS,), 0, 2), jax.random.fold_in(key_list[7], 1), 0, 1).astype(jnp.int32),
    }


def rotate(matrix, position):
    count = matrix.shape[0]
    split_heads = matrix.reshape(count, -1, HD)
    half_rot = ROT // 2
    inverse_freq = 10000.0 ** (-(jnp.arange(half_rot, dtype=jnp.float32) * 2.0 / ROT))
    angles = position.astype(jnp.float32)[:, None] * inverse_freq[None, :]
    cosine = jnp.cos(angles)[:, None, :]
    sine = jnp.sin(angles)[:, None, :]
    first_half = split_heads[..., :half_rot]
    second_half = split_heads[..., half_rot:ROT]
    rest_dims = split_heads[..., ROT:]
    turned = jnp.concatenate([first_half * cosine - second_half * sine, second_half * cosine + first_half * sine, rest_dims], axis=-1)
    return turned.reshape(count, -1)


def reference(queries, keys, values, pool_keys, pool_values, page_table, lengths, group_of):
    request_ends = jnp.cumsum(lengths).astype(jnp.int32)
    request_starts = (request_ends - lengths).astype(jnp.int32)
    token_rows = jnp.arange(TOKENS, dtype=jnp.int32)
    request_of = jnp.sum((token_rows[:, None] >= request_ends[None, :]).astype(jnp.int32), axis=1).astype(jnp.int32)
    offset_of = (token_rows - request_starts[request_of]).astype(jnp.int32)
    token_group = group_of[request_of]
    position = (PREFIX + offset_of).astype(jnp.int32)
    rot_queries = rotate(queries.astype(jnp.float32), position).astype(jnp.bfloat16)
    new_keys = rotate(keys.astype(jnp.float32), position).astype(jnp.bfloat16)
    slot_ids = jnp.arange(SLOTS, dtype=jnp.int32)
    slot_group = jnp.zeros((SLOTS,), jnp.int32).at[page_table].set((slot_ids >= PAGES_GROUP).astype(jnp.int32))
    key_group = jnp.repeat(slot_group, PAGE)
    pool_key_heads = pool_keys.reshape(SLOTS * PAGE, H, HD).astype(jnp.float32)
    pool_value_heads = pool_values.reshape(SLOTS * PAGE, H, HD).astype(jnp.float32)
    padded_keys = jnp.concatenate([jnp.zeros((TOK_DEV, C), jnp.bfloat16), new_keys], axis=0)
    padded_values = jnp.concatenate([jnp.zeros((TOK_DEV, C), jnp.bfloat16), values], axis=0)
    padded_request = jnp.concatenate([jnp.full((TOK_DEV,), -1, jnp.int32), request_of], axis=0)
    score_scale = HD ** -0.5

    def one_block(block_index):
        start = (block_index * TOK_DEV).astype(jnp.int32)
        query_block = lax.dynamic_slice_in_dim(rot_queries, start, TOK_DEV, 0).astype(jnp.float32).reshape(TOK_DEV, H, HD)
        query_request = lax.dynamic_slice_in_dim(request_of, start, TOK_DEV, 0)
        query_group = lax.dynamic_slice_in_dim(token_group, start, TOK_DEV, 0)
        near_keys = lax.dynamic_slice_in_dim(padded_keys, start, 2 * TOK_DEV, 0).astype(jnp.float32).reshape(2 * TOK_DEV, H, HD)
        near_values = lax.dynamic_slice_in_dim(padded_values, start, 2 * TOK_DEV, 0).astype(jnp.float32).reshape(2 * TOK_DEV, H, HD)
        near_request = lax.dynamic_slice_in_dim(padded_request, start, 2 * TOK_DEV, 0)
        key_rows = start - TOK_DEV + jnp.arange(2 * TOK_DEV, dtype=jnp.int32)
        query_rows = start + jnp.arange(TOK_DEV, dtype=jnp.int32)
        near_mask = (near_request[None, :] == query_request[:, None]) & (key_rows[None, :] <= query_rows[:, None])
        pool_mask = key_group[None, :] == query_group[:, None]
        all_keys = jnp.concatenate([pool_key_heads, near_keys], axis=0)
        all_values = jnp.concatenate([pool_value_heads, near_values], axis=0)
        allowed = jnp.concatenate([pool_mask, near_mask], axis=1)
        scores = jnp.einsum('qhd,khd->hqk', query_block, all_keys) * score_scale
        scores = jnp.where(allowed[None], scores, -1e30)
        row_max = jnp.max(scores, axis=-1, keepdims=True)
        weights = jnp.where(allowed[None], jnp.exp(scores - row_max), 0.0)
        total = jnp.sum(weights, axis=-1)
        weights_bf16 = lax.optimization_barrier(weights.astype(jnp.bfloat16)).astype(jnp.float32)
        output = jnp.einsum('hqk,khd->hqd', weights_bf16, all_values) / total[..., None]
        return output.transpose(1, 0, 2).reshape(TOK_DEV, C).astype(jnp.bfloat16)

    blocks = lax.map(one_block, jnp.arange(TOKENS // TOK_DEV, dtype=jnp.int32))
    context = blocks.reshape(TOKENS, C)
    return context, new_keys, values
```

```python
import functools

import jax
import jax.numpy as jnp
from jax import lax
from jax.experimental import pallas as pl
from jax.experimental.pallas import tpu as pltpu
from jax.sharding import PartitionSpec as P

HD = 96
ROT = 24
SLAB = 4
LOG2E = 1.4426950408889634
VMEM = pl.BlockSpec(memory_space=pltpu.VMEM)
SMEM = pl.BlockSpec(memory_space=pltpu.SMEM)
ANY = pl.BlockSpec(memory_space=pl.ANY)


def params(mib):
    return pltpu.CompilerParams(vmem_limit_bytes=mib << 20)


def shape(rows, lanes):
    return jax.ShapeDtypeStruct((rows, lanes), jnp.bfloat16)


def cost(flops, moved, exps=0):
    return pl.CostEstimate(flops=flops, bytes_accessed=moved, transcendentals=exps)


def starts_and_groups(rows, table):
    starts, ends, groups = table[0:1], table[1:2], table[2:3]
    start = jnp.max(jnp.where(ends <= rows, ends, 0.0), axis=1, keepdims=True)
    inside = (starts <= rows) & (rows < ends)
    group = jnp.sum(jnp.where(inside, groups, 0.0), axis=1, keepdims=True)
    return start, group


def lanes_at(ref, index, each, count, *lead):
    if each % 128 == 0:
        return ref[(*lead, slice(None), pl.ds(pl.multiple_of(index * each, each), each))]
    x = ref[(*lead, slice(None), slice(0, each))]
    for i in range(1, count):
        x = jnp.where(index == i, ref[(*lead, slice(None), slice(i * each, (i + 1) * each))], x)
    return x


def page_kernel(chunks, place, keys, values, *outs):
    lanes = keys.shape[-1] // SLAB
    half = lanes // chunks
    for n in range(SLAB):
        k = lanes_at(keys, place[1] ^ n, lanes, SLAB, 0)
        v = lanes_at(values, place[1] ^ n, lanes, SLAB, 0)
        for c in range(chunks):
            cut = slice(c * half, (c + 1) * half)
            pair = [k[:, cut], v[:, cut]]
            outs[c * SLAB + n][...] = jnp.concatenate(pair[::-1] if c else pair, axis=1)


def cut_page(place, keys, values, chunks):
    lanes = keys.shape[-1] // SLAB // chunks * 2
    outs = pl.pallas_call(
        functools.partial(page_kernel, chunks),
        out_shape=[shape(keys.shape[1], lanes)] * (SLAB * chunks),
        in_specs=[SMEM, VMEM, VMEM],
        out_specs=[VMEM] * (SLAB * chunks),
        compiler_params=params(16),
        cost_estimate=cost(0, 4 * keys.size),
    )(place, keys, values)
    return [outs[c * SLAB : (c + 1) * SLAB] for c in range(chunks)]


def rotate_kernel(tp, prefix, place, table, freq, queries, keys, values, *outs):
    rows, lanes = queries.shape[0], queries.shape[1] // tp
    width = freq.shape[1]
    token = place[2] + lax.broadcasted_iota(jnp.int32, (rows, 1), 0)
    token = token.astype(jnp.float32)
    start, _ = starts_and_groups(token, table[...])
    angle = (prefix + token - start) * freq[...]
    dim = lax.rem(lax.broadcasted_iota(jnp.int32, (rows, width), 1), HD)
    cosine, sine = jnp.cos(angle), jnp.sin(angle)
    keep = jnp.where(dim < ROT, cosine, 1.0)
    after = jnp.where(dim < ROT // 2, -sine, 0.0)
    before = jnp.where((dim >= ROT // 2) & (dim < ROT), sine, 0.0)
    for m in range(tp):
        base = (place[3] ^ m) * lanes
        for part in range(lanes // width):
            at = pl.ds(pl.multiple_of(base + part * width, width), width)
            to = pl.ds(part * width, width)
            for source, out in ((queries, outs[m]), (keys, outs[tp + m])):
                x = source[:, at].astype(jnp.float32)
                far = pltpu.roll(x, width - ROT // 2, 1)
                near = pltpu.roll(x, ROT // 2, 1)
                out[:, to] = (x * keep + far * after + near * before).astype(jnp.bfloat16)
            outs[2 * tp + m][:, to] = values[:, at]


def rotate_and_cut(place, table, freq, queries, keys, values, tp, prefix):
    rows, lanes = queries.shape[0], queries.shape[1] // tp
    outs = pl.pallas_call(
        functools.partial(rotate_kernel, tp, prefix),
        out_shape=[shape(rows, lanes)] * (3 * tp),
        in_specs=[SMEM] + [VMEM] * 5,
        out_specs=[VMEM] * (3 * tp),
        compiler_params=params(24),
        cost_estimate=cost(0, 12 * queries.size),
    )(place, table, freq, queries, keys, values)
    return outs[:tp], outs[tp : 2 * tp], outs[2 * tp :]


def query_kernel(tp, place, *refs):
    parts, outs = refs[:tp], refs[tp:]
    rows, lanes = parts[0].shape[0], outs[0].shape[1]
    for m in range(tp):
        to = pl.ds(pl.multiple_of((place[3] ^ m) * rows, rows), rows)
        for n in range(SLAB):
            outs[n][to, :] = lanes_at(parts[m], place[1] ^ n, lanes, SLAB)


def cut_queries(place, parts):
    tp = len(parts)
    rows, lanes = parts[0].shape
    return pl.pallas_call(
        functools.partial(query_kernel, tp),
        out_shape=[shape(rows * tp, lanes // SLAB)] * SLAB,
        in_specs=[SMEM] + [VMEM] * tp,
        out_specs=[VMEM] * SLAB,
        compiler_params=params(16),
        cost_estimate=cost(0, 4 * tp * parts[0].size),
    )(place, *parts)


def suffix_kernel(tp, chunks, place, *refs):
    keys, values = refs[:tp], refs[tp : 2 * tp]
    new_keys, new_values = refs[2 * tp : 2 * tp + 2]
    outs = refs[2 * tp + 2 :]
    rows, lanes = keys[0].shape[0], new_keys.shape[1] // SLAB
    for m in range(tp):
        to = pl.ds(pl.multiple_of((place[3] ^ m) * rows, rows), rows)
        new_keys[to, :] = keys[m][...]
        new_values[to, :] = values[m][...]
        for n in range(SLAB):
            k = lanes_at(keys[m], place[1] ^ n, lanes, SLAB)
            v = lanes_at(values[m], place[1] ^ n, lanes, SLAB)
            half = lanes // 2
            parts = [k, v[:, half:], v[:, :half]] if chunks == 2 else [k, v]
            outs[n][to, :] = jnp.concatenate(parts, axis=1)


def cut_suffix(place, keys, values, chunks):
    tp = len(keys)
    rows, lanes = keys[0].shape
    outs = pl.pallas_call(
        functools.partial(suffix_kernel, tp, chunks),
        out_shape=[shape(rows * tp, lanes)] * 2 + [shape(rows * tp, lanes // SLAB * 2)] * SLAB,
        in_specs=[SMEM] + [VMEM] * (2 * tp),
        out_specs=[VMEM] * (2 + SLAB),
        compiler_params=params(24),
        cost_estimate=cost(0, 12 * tp * keys[0].size),
    )(place, *keys, *values)
    return outs[0], outs[1], outs[2:]


def window(lane, count, lanes):
    return lane // 128 * 128, min(-(-(lane + count) // 128) * 128, lanes)


def attend_kernel(plan, place, pages, table, *refs):
    chunk, heads, lines, early_count, unit_count, page, block = plan
    q_parts, kv_parts = refs[:SLAB], refs[SLAB : 2 * SLAB]
    early = refs[2 * SLAB : 2 * SLAB + early_count]
    units = refs[2 * SLAB + early_count : 2 * SLAB + early_count + unit_count]
    refs = refs[2 * SLAB + early_count + unit_count :]
    outs, (q_all, kv_all, pool, seat, sems) = refs[:SLAB], refs[SLAB:]
    z, j = place[0], place[1]
    slots = lines * SLAB
    middle = (z > 0) & (z < lines - 1)
    copies = []

    def start(source, target, other=None, take_other=None):
        sem = sems.at[len(copies)]
        copy = pltpu.make_async_copy(source, target, sem)
        if other is None:
            copy.start()
        else:
            pl.when(jnp.logical_not(take_other))(copy.start)
            pl.when(take_other)(pltpu.make_async_copy(other, target, sem).start)
        copies.append(copy)

    def fill(i, carry):
        seat[pages[i]] = i
        return carry

    lax.fori_loop(0, slots, fill, 0)
    for n in range(SLAB):
        at = pl.multiple_of((j ^ n) * block, block)
        start(q_parts[n], q_all.at[pl.ds(at, block)])
        start(kv_parts[n], kv_all.at[pl.ds(at + block, block)])
    before = kv_all.at[pl.ds(0, block)]
    if early_count == 2:
        start(early[0], before, early[1], z == 2)
    else:
        start(early[0], before)
    if unit_count == 6:
        own, a1, b1, a2, b2, a3 = units
        third, fourth = jnp.where(z < 2, 2, 1), jnp.where(z < 2, 3, 0)
        sources = [(own, None, z, 0), (a1, None, z ^ 1, 0), (a2, b1, third, 0), (a3, b2, fourth, 0)]
    else:
        sources = [(units[0], None, line, line * SLAB * page) for line in range(lines)]
    for source, other, line, base in sources:
        for n in range(SLAB):
            rows = pl.ds(base + n * page, page)
            to = pl.multiple_of(seat[line * SLAB + (j ^ n)] * page, page)
            target = pool.at[pl.ds(to, page)]
            if other is None:
                start(source.at[rows], target)
            else:
                start(source.at[rows], target, other.at[rows], middle)
    for copy in copies:
        copy.wait()

    half = slots // 2 * page
    own_lanes = q_all.shape[1]
    width = heads * HD
    key_lane = chunk * width
    value_lane = (key_lane + width) % (2 * width)
    key_low, key_high = window(key_lane, width, 2 * own_lanes)
    low, high = window(value_lane, width, 2 * width)
    near_low = low + (own_lanes if 2 * width == own_lanes else 0)
    key_at, value_at = slice(key_low, key_high), slice(low, high)
    near_at = slice(near_low, near_low + high - low)
    factor = HD ** (-0.5) * LOG2E
    contract = (((1,), (1,)), ((), ()))
    first = z * (SLAB * block)

    def dot_t(x, y):
        return lax.dot_general(x, y, contract, preferred_element_type=jnp.float32)

    def dot(x, y):
        return jnp.dot(x, y, preferred_element_type=jnp.float32)

    def one_block(n, carry):
        b = j ^ n
        rows = pl.ds(pl.multiple_of(b * block, block), block)
        token = first + b * block + lax.broadcasted_iota(jnp.int32, (block, 1), 0)
        request_start, group = starts_and_groups(token.astype(jnp.float32), table[...])
        zero_group = group < 0.5
        key = first + (b - 1) * block + lax.broadcasted_iota(jnp.int32, (block, 2 * block), 1)
        near = (key >= request_start.astype(jnp.int32)) & (key <= token)
        near_rows = pl.ds(pl.multiple_of(b * block, block), 2 * block)
        query_high = min(key_high, own_lanes)
        queries = q_all[rows, key_low:query_high]
        lane = key_low + lax.broadcasted_iota(jnp.int32, queries.shape, 1)
        out_lane = low + lax.broadcasted_iota(jnp.int32, (block, high - low), 1)
        result = jnp.zeros((block, high - low), jnp.float32)
        for h in range(heads):
            begin = key_lane + h * HD
            query = jnp.where((lane >= begin) & (lane < begin + HD), queries, jnp.zeros_like(queries))
            if query_high < key_high:
                rest = jnp.zeros((block, key_high - query_high), query.dtype)
                query = jnp.concatenate([query, rest], axis=1)
            score = jnp.where(
                zero_group,
                dot_t(query, pool[0:half, key_at]),
                dot_t(query, pool[half : 2 * half, key_at]),
            )
            near_score = jnp.where(near, dot_t(query, kv_all[near_rows, key_at]), -1e30)
            top = jnp.maximum(
                jnp.max(score, axis=1, keepdims=True), jnp.max(near_score, axis=1, keepdims=True)
            )
            weight = jnp.exp2((score - top) * factor)
            near_weight = jnp.exp2((near_score - top) * factor)
            total = jnp.sum(weight, axis=1, keepdims=True) + jnp.sum(
                near_weight, axis=1, keepdims=True
            )
            narrow = weight.astype(jnp.bfloat16)
            nothing = jnp.zeros_like(narrow)
            mixed = (
                dot(jnp.where(zero_group, narrow, nothing), pool[0:half, value_at])
                + dot(jnp.where(zero_group, nothing, narrow), pool[half : 2 * half, value_at])
                + dot(near_weight.astype(jnp.bfloat16), kv_all[near_rows, near_at])
            )
            begin = value_lane + h * HD
            inside = (out_lane >= begin) & (out_lane < begin + HD)
            result = jnp.where(inside, mixed / total, result)
        result = result[:, value_lane - low : value_lane - low + width].astype(jnp.bfloat16)
        folded = jnp.concatenate([result[: block // 2], result[block // 2 :]], axis=1)
        for i in range(SLAB):

            @pl.when(n == i)
            def _():
                outs[i][...] = folded

        return carry

    lax.fori_loop(0, SLAB, one_block, 0)


def attend(place, pages, table, q_parts, kv_parts, early, units, chunk, chunks, lines, page):
    block, own_lanes = q_parts[0].shape
    heads = own_lanes // HD // chunks
    slots = lines * SLAB
    pool_lanes = 2 * heads * HD
    plan = (chunk, heads, lines, len(early), len(units), page, block)
    keys = slots * page + 2 * block
    copies = 2 * SLAB + 1 + slots
    return pl.pallas_call(
        functools.partial(attend_kernel, plan),
        out_shape=[shape(block // 2, pool_lanes)] * SLAB,
        in_specs=[SMEM, SMEM, VMEM] + [ANY] * (2 * SLAB + len(early) + len(units)),
        out_specs=[VMEM] * SLAB,
        scratch_shapes=[
            pltpu.VMEM((SLAB * block, own_lanes), jnp.bfloat16),
            pltpu.VMEM(((SLAB + 1) * block, 2 * own_lanes), jnp.bfloat16),
            pltpu.VMEM((slots * page, pool_lanes), jnp.bfloat16),
            pltpu.SMEM((slots,), jnp.int32),
            pltpu.SemaphoreType.DMA((copies,)),
        ],
        compiler_params=params(32),
        cost_estimate=cost(
            4 * SLAB * block * keys * heads * 256,
            2 * keys * pool_lanes,
            SLAB * block * heads * (keys // 2),
        ),
    )(place, pages, table, *q_parts, *kv_parts, *early, *units)


def back_kernel(tp, place, *refs):
    parts, outs = refs[:SLAB], refs[SLAB:]
    rows, lanes = parts[0].shape
    each = 2 * rows // tp
    for m in range(tp):
        first = (place[3] ^ m) * each
        upper = first >= rows
        at = pl.ds(pl.multiple_of(jnp.where(upper, first - rows, first), each), each)
        cuts = []
        for n in range(SLAB):
            x = parts[n][at, :]
            cuts.append(jnp.where(upper, x[:, lanes // 2 :], x[:, : lanes // 2]))
        outs[m][...] = jnp.concatenate(cuts, axis=1)


def cut_back(place, parts, tp):
    rows, lanes = parts[0].shape
    return pl.pallas_call(
        functools.partial(back_kernel, tp),
        out_shape=[shape(2 * rows // tp, lanes // 2 * SLAB)] * tp,
        in_specs=[SMEM] + [VMEM] * SLAB,
        out_specs=[VMEM] * tp,
        compiler_params=params(16),
        cost_estimate=cost(0, 4 * SLAB * rows * lanes),
    )(place, *parts)


def join_kernel(tp, chunks, place, *refs):
    out = refs[-1]
    lanes = out.shape[1] // tp
    each = lanes // SLAB
    cut = each // chunks
    for m in range(tp):
        for n in range(SLAB):
            base = (place[3] ^ m) * lanes + (place[1] ^ n) * each
            pieces = [refs[c * tp + m][:, n * cut : (n + 1) * cut] for c in range(chunks)]
            x = jnp.concatenate(pieces, axis=1) if chunks > 1 else pieces[0]
            if each % 128:
                for i in range(tp * SLAB):

                    @pl.when(base == i * each)
                    def _():
                        out[:, i * each : (i + 1) * each] = x
            else:
                out[:, pl.ds(pl.multiple_of(base, each), each)] = x


def join(place, parts, tp, chunks):
    rows, lanes = parts[0][0].shape
    return pl.pallas_call(
        functools.partial(join_kernel, tp, chunks),
        out_shape=shape(rows, lanes * tp * chunks),
        in_specs=[SMEM] + [VMEM] * (tp * chunks),
        out_specs=VMEM,
        compiler_params=params(16),
        cost_estimate=cost(0, 4 * rows * lanes * tp * chunks),
    )(place, *[x for chunk in parts for x in chunk])


def swap(parts, axis):
    size = lax.axis_size(axis)
    return [parts[0]] + [
        lax.ppermute(parts[m], axis, [(i, i ^ m) for i in range(size)])
        for m in range(1, len(parts))
    ]


def along(block, pairs):
    return lax.ppermute(
        block, "seq", [(a * SLAB + j, b * SLAB + j) for a, b in pairs for j in range(SLAB)]
    )


INNER = [(1, 2), (2, 1)]
OUTER = [(0, 1), (1, 0), (2, 3), (3, 2)]
OUTWARD = [(1, 0), (2, 3)]


def gather(unit, lines):
    if lines == 4:
        a1 = along(unit, OUTER)
        b1 = along(unit, INNER)
        b2 = along(a1, INNER)
        a2 = along(b1, OUTWARD)
        a3 = along(b2, OUTWARD)
        return [unit, a1, b1, a2, b2, a3]
    groups = [[line * SLAB + j for line in range(lines)] for j in range(SLAB)]
    return [lax.all_gather(unit, "seq", axis=0, axis_index_groups=groups, tiled=True)]


def local(queries, keys, values, pool_keys, pool_values, page_table, lengths, group_of):
    seq, tp = lax.axis_size("seq"), lax.axis_size("tp")
    lines = seq // SLAB
    rows = queries.shape[0]
    page = pool_keys.shape[1]
    own_heads = pool_keys.shape[2] // SLAB // HD
    chunks = 2 if own_heads % 2 == 0 else 1
    index, y = lax.axis_index("seq"), lax.axis_index("tp")
    j = index % SLAB
    place = jnp.stack([index // SLAB, j, (index * tp + y) * rows, y]).astype(jnp.int32)
    ends = jnp.cumsum(lengths)
    table = jnp.stack([ends - lengths, ends, group_of]).astype(jnp.float32)
    width = pool_keys.shape[2] // SLAB
    if width % 128:
        width = pool_keys.shape[2]
    dims = (jnp.arange(width) % HD) % (ROT // 2)
    freq = (10000.0 ** (-(dims.astype(jnp.float32) * 2.0 / ROT)))[None]
    prefix = seq // 2 * page

    pieces = cut_page(place, pool_keys, pool_values, chunks)
    q_cut, k_cut, v_cut = rotate_and_cut(place, table, freq, queries, keys, values, tp, prefix)
    units = [
        gather(jnp.concatenate(swap(pieces[c], "seq"), axis=0), lines) for c in range(chunks)
    ]
    q_parts = swap(cut_queries(place, swap(q_cut, "tp")), "seq")
    new_keys, new_values, kv_cut = cut_suffix(place, swap(k_cut, "tp"), swap(v_cut, "tp"), chunks)
    kv_parts = swap(kv_cut, "seq")
    last = lax.select_n(jnp.broadcast_to(j ^ (SLAB - 1), ()), *kv_parts)
    if lines == 4:
        early = [along(last, [(0, 1), (2, 3)]), along(last, [(1, 2)])]
    else:
        early = [along(last, [(i, i + 1) for i in range(lines - 1)])]
    backs = []
    for c in range(chunks):
        outs = attend(
            place, page_table, table, q_parts, kv_parts, early, units[c], c, chunks, lines, page
        )
        backs.append(swap(cut_back(place, swap(outs, "seq"), tp), "tp"))
    return join(place, backs, tp, chunks), new_keys, new_values


def solution(mesh):
    return jax.shard_map(
        local,
        mesh=mesh,
        in_specs=(
            P(("seq", "tp"), None),
            P(("seq", "tp"), None),
            P(("seq", "tp"), None),
            P("seq", None, "tp"),
            P("seq", None, "tp"),
            P(),
            P(),
            P(),
        ),
        out_specs=(P(("seq", "tp"), None), P("seq", "tp"), P("seq", "tp")),
        check_vma=False,
    )
```

```python
import functools

import jax
import jax.numpy as jnp
from jax import lax
from jax.experimental import pallas as pl
from jax.experimental.pallas import tpu as pltpu
from jax.sharding import PartitionSpec as P

HD = 96
ROT = 24
SLAB = 4
LOG2E = 1.4426950408889634
VMEM = pl.BlockSpec(memory_space=pltpu.VMEM)
SMEM = pl.BlockSpec(memory_space=pltpu.SMEM)


def params(mib):
    return pltpu.CompilerParams(vmem_limit_bytes=mib << 20)


def shape(rows, lanes):
    return jax.ShapeDtypeStruct((rows, lanes), jnp.bfloat16)


def cost(flops, moved, exps=0):
    return pl.CostEstimate(flops=1, bytes_accessed=1, transcendentals=0)


def starts_and_groups(rows, table):
    starts, ends, groups = table[0:1], table[1:2], table[2:3]
    start = jnp.max(jnp.where(ends <= rows, ends, 0.0), axis=1, keepdims=True)
    inside = (starts <= rows) & (rows < ends)
    group = jnp.sum(jnp.where(inside, groups, 0.0), axis=1, keepdims=True)
    return start, group


def lanes_at(ref, index, each, count, *lead):
    if each % 128 == 0:
        return ref[(*lead, slice(None), pl.ds(pl.multiple_of(index * each, each), each))]
    x = ref[(*lead, slice(None), slice(0, each))]
    for i in range(1, count):
        x = jnp.where(index == i, ref[(*lead, slice(None), slice(i * each, (i + 1) * each))], x)
    return x


def page_kernel(chunks, place, keys, values, *outs):
    lanes = keys.shape[-1] // SLAB
    half = lanes // chunks
    for n in range(SLAB):
        k = lanes_at(keys, place[1] ^ n, lanes, SLAB, 0)
        v = lanes_at(values, place[1] ^ n, lanes, SLAB, 0)
        for c in range(chunks):
            cut = slice(c * half, (c + 1) * half)
            pair = [k[:, cut], v[:, cut]]
            outs[c * SLAB + n][...] = jnp.concatenate(pair[::-1] if c else pair, axis=1)


def cut_page(place, keys, values, chunks):
    lanes = keys.shape[-1] // SLAB // chunks * 2
    outs = pl.pallas_call(
        functools.partial(page_kernel, chunks),
        out_shape=[shape(keys.shape[1], lanes)] * (SLAB * chunks),
        in_specs=[SMEM, VMEM, VMEM],
        out_specs=[VMEM] * (SLAB * chunks),
        compiler_params=params(16),
        cost_estimate=cost(0, 4 * keys.size),
    )(place, keys, values)
    return [outs[c * SLAB : (c + 1) * SLAB] for c in range(chunks)]


def rotate_kernel(tp, chunks, prefix, place, table, freq, queries, keys, values, *outs):
    rows, lanes = queries.shape[0], queries.shape[1] // tp
    width = freq.shape[1]
    token = place[2] + lax.broadcasted_iota(jnp.int32, (rows, 1), 0)
    token = token.astype(jnp.float32)
    start, _ = starts_and_groups(token, table[...])
    angle = (prefix + token - start) * freq[...]
    dim = lax.rem(lax.broadcasted_iota(jnp.int32, (rows, width), 1), HD)
    cosine, sine = jnp.cos(angle), jnp.sin(angle)
    keep = jnp.where(dim < ROT, cosine, 1.0)
    after = jnp.where(dim < ROT // 2, -sine, 0.0)
    before = jnp.where((dim >= ROT // 2) & (dim < ROT), sine, 0.0)
    cut = width // chunks

    def turned(x):
        x = x.astype(jnp.float32)
        far = pltpu.roll(x, width - ROT // 2, 1)
        near = pltpu.roll(x, ROT // 2, 1)
        return (x * keep + far * after + near * before).astype(jnp.bfloat16)

    for m in range(tp):
        base = (place[3] ^ m) * lanes
        for part in range(lanes // width):
            at = pl.ds(pl.multiple_of(base + part * width, width), width)
            q, k, v = turned(queries[:, at]), turned(keys[:, at]), values[:, at]
            quarters = lanes // width == 1 and SLAB or 1
            for i in range(quarters):
                for c in range(chunks):
                    size = cut // quarters
                    of = slice(c * cut + i * size, c * cut + (i + 1) * size)
                    to = slice((part + i) * 2 * size, (part + i + 1) * 2 * size)
                    pair = [k[:, of], v[:, of]]
                    out = outs[c * tp + m]
                    out[:rows, to] = jnp.concatenate(pair[::-1] if c else pair, axis=1)
                    out[rows:, to] = jnp.concatenate([q[: rows // 2, of], q[rows // 2 :, of]], axis=1)


def rotate_and_cut(place, table, freq, queries, keys, values, tp, chunks, prefix):
    rows, lanes = queries.shape[0], queries.shape[1] // tp
    outs = pl.pallas_call(
        functools.partial(rotate_kernel, tp, chunks, prefix),
        out_shape=[shape(rows * 3 // 2, 2 * lanes // chunks)] * (chunks * tp),
        in_specs=[SMEM] + [VMEM] * 5,
        out_specs=[VMEM] * (chunks * tp),
        compiler_params=params(24),
        cost_estimate=cost(0, 12 * queries.size),
    )(place, table, freq, queries, keys, values)
    return [outs[c * tp : (c + 1) * tp] for c in range(chunks)]


def quarter_kernel(tp, place, *refs):
    parts, outs = refs[:tp], refs[tp:]
    rows, each = parts[0].shape[0] * 2 // 3, outs[0].shape[1]
    for n in range(SLAB):
        for m in range(tp):
            x = lanes_at(parts[m], place[1] ^ n, each, SLAB)
            to = pl.multiple_of((place[3] ^ m) * rows, rows)
            outs[n][pl.ds(to, rows), :] = x[:rows]
            to = pl.multiple_of(tp * rows + (place[3] ^ m) * (rows // 2), rows // 2)
            outs[n][pl.ds(to, rows // 2), :] = x[rows:]


def cut_quarters(place, parts):
    tp = len(parts)
    rows, lanes = parts[0].shape
    return pl.pallas_call(
        functools.partial(quarter_kernel, tp),
        out_shape=[shape(rows * tp, lanes // SLAB)] * SLAB,
        in_specs=[SMEM] + [VMEM] * tp,
        out_specs=[VMEM] * SLAB,
        compiler_params=params(24),
        cost_estimate=cost(0, 4 * tp * parts[0].size),
    )(place, *parts)


def output_kernel(tp, chunks, place, *refs):
    parts, outs = refs[: chunks * tp], refs[chunks * tp :]
    rows, lanes = outs[0].shape[0] // tp, outs[0].shape[1]
    each = lanes // chunks // SLAB
    for m in range(tp):
        to = pl.ds(pl.multiple_of((place[3] ^ m) * rows, rows), rows)
        for section, out in enumerate(outs):
            pieces = []
            for i in range(SLAB):
                for c in range(chunks):
                    at = 2 * i * each + (each if section != c else 0)
                    pieces.append(parts[c * tp + m][:rows, at : at + each])
            out[to, :] = jnp.concatenate(pieces, axis=1)


def join_outputs(place, parts, lanes):
    chunks, tp = len(parts), len(parts[0])
    rows = parts[0][0].shape[0] * 2 // 3
    return pl.pallas_call(
        functools.partial(output_kernel, tp, chunks),
        out_shape=[shape(rows * tp, lanes)] * 2,
        in_specs=[SMEM] + [VMEM] * (tp * chunks),
        out_specs=[VMEM] * 2,
        compiler_params=params(24),
        cost_estimate=cost(0, 8 * rows * tp * lanes),
    )(place, *[x for chunk in parts for x in chunk])


def stack_kernel(*refs):
    rows = refs[0].shape[0]
    for n, ref in enumerate(refs[:-1]):
        refs[-1][n * rows : (n + 1) * rows, :] = ref[...]


def stacked(parts):
    rows, lanes = parts[0].shape
    return pl.pallas_call(
        stack_kernel,
        out_shape=shape(rows * len(parts), lanes),
        in_specs=[VMEM] * len(parts),
        out_specs=VMEM,
        compiler_params=params(16),
        cost_estimate=cost(0, 4 * len(parts) * parts[0].size),
    )(*parts)


def last_kernel(place, *refs):
    out = refs[-1]
    for n in range(SLAB):

        @pl.when((place[1] ^ n) == SLAB - 1)
        def _():
            out[...] = refs[n][: out.shape[0], :]


def last_of(place, parts, block):
    return pl.pallas_call(
        last_kernel,
        out_shape=shape(block, parts[0].shape[1]),
        in_specs=[SMEM] + [VMEM] * SLAB,
        out_specs=VMEM,
        compiler_params=params(16),
        cost_estimate=cost(0, 4 * block * parts[0].shape[1]),
    )(place, *parts)


def window(lane, count, lanes):
    return lane // 128 * 128, min(-(-(lane + count) // 128) * 128, lanes)


def set_in(x, offset, lanes):
    rows, count = x.shape
    parts = [x]
    if offset:
        parts.insert(0, jnp.zeros((rows, offset), x.dtype))
    if lanes > offset + count:
        parts.append(jnp.zeros((rows, lanes - offset - count), x.dtype))
    return jnp.concatenate(parts, axis=1) if len(parts) > 1 else x


def attend_kernel(plan, place, pages, table, *refs):
    chunk, heads, lines, early_count, unit_count, page, block, rows = plan
    parts = refs[:SLAB]
    early = refs[SLAB : SLAB + early_count]
    units = refs[SLAB + early_count : SLAB + early_count + unit_count]
    refs = refs[SLAB + early_count + unit_count :]
    outs, (near_keys, near_values, pool, seat) = refs[:SLAB], refs[SLAB:]
    z, j = place[0], place[1]
    slots = lines * SLAB
    middle = (z > 0) & (z < lines - 1)

    half = slots // 2 * page
    width = heads * HD
    key_lane = width if chunk else 0
    value_lane = width - key_lane
    key_low, key_high = window(key_lane, width, 2 * width)
    low, high = window(value_lane, width, 2 * width)
    key_at, value_at = slice(key_low, key_high), slice(low, high)
    factor = HD ** (-0.5) * LOG2E
    contract = (((1,), (1,)), ((), ()))
    first = z * (SLAB * block)

    def dot_t(x, y):
        return lax.dot_general(x, y, contract, preferred_element_type=jnp.float32)

    def dot(x, y):
        return jnp.dot(x, y, preferred_element_type=jnp.float32)

    def fill(i, carry):
        seat[pages[i]] = i
        return carry

    lax.fori_loop(0, slots, fill, 0)

    def set_near(source, at):
        near_keys[pl.ds(at, block), :] = source[:block, key_at]
        near_values[pl.ds(at, block), :] = source[:block, value_at]

    def set_pool(source, line, base):
        for n in range(SLAB):
            to = pl.multiple_of(seat[line * SLAB + (j ^ n)] * page, page)
            pool[pl.ds(to, page), :] = source[base + n * page : base + (n + 1) * page, :]

    for n in range(SLAB):
        set_near(parts[n], pl.multiple_of(((j ^ n) + 1) * block, block))
    if early_count == 2:
        pl.when(z == 2)(lambda: set_near(early[1], 0))
        pl.when(z != 2)(lambda: set_near(early[0], 0))
    else:
        set_near(early[0], 0)
    if unit_count == 6:
        own, a1, b1, a2, b2, a3 = units
        set_pool(own, z, 0)
        set_pool(a1, z ^ 1, 0)
        third, fourth = jnp.where(z < 2, 2, 1), jnp.where(z < 2, 3, 0)

        @pl.when(middle)
        def _():
            set_pool(b1, third, 0)
            set_pool(b2, fourth, 0)

        @pl.when(jnp.logical_not(middle))
        def _():
            set_pool(a2, third, 0)
            set_pool(a3, fourth, 0)
    else:
        for line in range(lines):
            set_pool(units[0], line, line * SLAB * page)

    for n in range(SLAB):
        b = j ^ n
        token = first + b * block + lax.broadcasted_iota(jnp.int32, (block, 1), 0)
        request_start, group = starts_and_groups(token.astype(jnp.float32), table[...])
        zero_group = group < 0.5
        key = first + (b - 1) * block + lax.broadcasted_iota(jnp.int32, (block, 2 * block), 1)
        near = (key >= request_start.astype(jnp.int32)) & (key <= token)
        near_rows = pl.ds(pl.multiple_of(b * block, block), 2 * block)
        folded = parts[n][block:, :]
        halves = []
        for at in range(0, block // 2, rows // 2):
            some = folded[at : at + rows // 2]
            halves += [some[:, :width], some[:, width:]]
        queries = jnp.concatenate(halves, axis=0)
        queries = set_in(queries, key_lane - key_low, key_high - key_low)
        lane = key_low + lax.broadcasted_iota(jnp.int32, queries.shape, 1)
        out_lane = low + lax.broadcasted_iota(jnp.int32, (block, high - low), 1)
        result = jnp.zeros((block, high - low), jnp.float32)
        for h in range(heads):
            begin = key_lane + h * HD
            query = jnp.where((lane >= begin) & (lane < begin + HD), queries, jnp.zeros_like(queries))
            score = jnp.where(
                zero_group,
                dot_t(query, pool[0:half, key_at]),
                dot_t(query, pool[half : 2 * half, key_at]),
            )
            near_score = jnp.where(near, dot_t(query, near_keys[near_rows, :]), -1e30)
            top = jnp.maximum(
                jnp.max(score, axis=1, keepdims=True), jnp.max(near_score, axis=1, keepdims=True)
            )
            weight = jnp.exp2((score - top) * factor)
            near_weight = jnp.exp2((near_score - top) * factor)
            total = jnp.sum(weight, axis=1, keepdims=True) + jnp.sum(
                near_weight, axis=1, keepdims=True
            )
            narrow = weight.astype(jnp.bfloat16)
            nothing = jnp.zeros_like(narrow)
            mixed = (
                dot(jnp.where(zero_group, narrow, nothing), pool[0:half, value_at])
                + dot(jnp.where(zero_group, nothing, narrow), pool[half : 2 * half, value_at])
                + dot(near_weight.astype(jnp.bfloat16), near_values[near_rows, :])
            )
            begin = value_lane + h * HD
            inside = (out_lane >= begin) & (out_lane < begin + HD)
            result = jnp.where(inside, mixed / total, result)
        result = result[:, value_lane - low : value_lane - low + width].astype(jnp.bfloat16)
        folded = jnp.concatenate([result[: block // 2], result[block // 2 :]], axis=1)
        outs[n][...] = folded


def attend(place, pages, table, parts, early, units, chunk, lines, page, rows):
    block, width = parts[0].shape[0] * 2 // 3, parts[0].shape[1] // 2
    heads = width // HD
    slots = lines * SLAB
    key_low, key_high = window(width if chunk else 0, width, 2 * width)
    low, high = window(0 if chunk else width, width, 2 * width)
    plan = (chunk, heads, lines, len(early), len(units), page, block, rows)
    keys = slots * page + 2 * block
    return pl.pallas_call(
        functools.partial(attend_kernel, plan),
        out_shape=[shape(block // 2, 2 * width)] * SLAB,
        in_specs=[SMEM, SMEM, VMEM] + [VMEM] * (SLAB + len(early) + len(units)),
        out_specs=[VMEM] * SLAB,
        scratch_shapes=[
            pltpu.VMEM(((SLAB + 1) * block, key_high - key_low), jnp.bfloat16),
            pltpu.VMEM(((SLAB + 1) * block, high - low), jnp.bfloat16),
            pltpu.VMEM((slots * page, 2 * width), jnp.bfloat16),
            pltpu.SMEM((slots,), jnp.int32),
        ],
        compiler_params=params(32),
        cost_estimate=cost(
            4 * SLAB * block * keys * heads * 256,
            4 * keys * width,
            SLAB * block * heads * (keys // 2),
        ),
    )(place, pages, table, *parts, *early, *units)


def back_kernel(tp, place, *refs):
    parts, outs = refs[:SLAB], refs[SLAB:]
    rows, lanes = parts[0].shape
    each = 2 * rows // tp
    for m in range(tp):
        first = (place[3] ^ m) * each
        upper = first >= rows
        at = pl.ds(pl.multiple_of(jnp.where(upper, first - rows, first), each), each)
        cuts = []
        for n in range(SLAB):
            x = parts[n][at, :]
            cuts.append(jnp.where(upper, x[:, lanes // 2 :], x[:, : lanes // 2]))
        outs[m][...] = jnp.concatenate(cuts, axis=1)


def cut_back(place, parts, tp):
    rows, lanes = parts[0].shape
    return pl.pallas_call(
        functools.partial(back_kernel, tp),
        out_shape=[shape(2 * rows // tp, lanes // 2 * SLAB)] * tp,
        in_specs=[SMEM] + [VMEM] * SLAB,
        out_specs=[VMEM] * tp,
        compiler_params=params(16),
        cost_estimate=cost(0, 4 * SLAB * rows * lanes),
    )(place, *parts)


def join_kernel(tp, chunks, place, *refs):
    out = refs[-1]
    lanes = out.shape[1] // tp
    each = lanes // SLAB
    cut = each // chunks
    for m in range(tp):
        for n in range(SLAB):
            base = (place[3] ^ m) * lanes + (place[1] ^ n) * each
            pieces = [refs[c * tp + m][:, n * cut : (n + 1) * cut] for c in range(chunks)]
            x = jnp.concatenate(pieces, axis=1) if chunks > 1 else pieces[0]
            if each % 128:
                for i in range(tp * SLAB):

                    @pl.when(base == i * each)
                    def _():
                        out[:, i * each : (i + 1) * each] = x
            else:
                out[:, pl.ds(pl.multiple_of(base, each), each)] = x


def join(place, parts, tp, chunks):
    rows, lanes = parts[0][0].shape
    return pl.pallas_call(
        functools.partial(join_kernel, tp, chunks),
        out_shape=shape(rows, lanes * tp * chunks),
        in_specs=[SMEM] + [VMEM] * (tp * chunks),
        out_specs=VMEM,
        compiler_params=params(16),
        cost_estimate=cost(0, 4 * rows * lanes * tp * chunks),
    )(place, *[x for chunk in parts for x in chunk])


def swap(parts, axis):
    size = lax.axis_size(axis)
    return [parts[0]] + [
        lax.ppermute(parts[m], axis, [(i, i ^ m) for i in range(size)])
        for m in range(1, len(parts))
    ]


def along(block, pairs):
    return lax.ppermute(
        block, "seq", [(a * SLAB + j, b * SLAB + j) for a, b in pairs for j in range(SLAB)]
    )


INNER = [(1, 2), (2, 1)]
OUTER = [(0, 1), (1, 0), (2, 3), (3, 2)]
OUTWARD = [(1, 0), (2, 3)]


def gather(unit, lines):
    if lines == 4:
        a1 = along(unit, OUTER)
        b1 = along(unit, INNER)
        b2 = along(a1, INNER)
        a2 = along(b1, OUTWARD)
        a3 = along(b2, OUTWARD)
        return [unit, a1, b1, a2, b2, a3]
    groups = [[line * SLAB + j for line in range(lines)] for j in range(SLAB)]
    return [lax.all_gather(unit, "seq", axis=0, axis_index_groups=groups, tiled=True)]


def local(queries, keys, values, pool_keys, pool_values, page_table, lengths, group_of):
    seq, tp = lax.axis_size("seq"), lax.axis_size("tp")
    lines = seq // SLAB
    rows = queries.shape[0]
    page = pool_keys.shape[1]
    own_heads = pool_keys.shape[2] // SLAB // HD
    chunks = 2 if own_heads % 2 == 0 else 1
    index, y = lax.axis_index("seq"), lax.axis_index("tp")
    j = index % SLAB
    place = jnp.stack([index // SLAB, j, (index * tp + y) * rows, y]).astype(jnp.int32)
    ends = jnp.cumsum(lengths)
    table = jnp.stack([ends - lengths, ends, group_of]).astype(jnp.float32)
    width = pool_keys.shape[2] // SLAB
    if width % 128:
        width = pool_keys.shape[2]
    dims = (jnp.arange(width) % HD) % (ROT // 2)
    freq = (10000.0 ** (-(dims.astype(jnp.float32) * 2.0 / ROT)))[None]
    prefix = seq // 2 * page

    after = lax.optimization_barrier
    after = lax.optimization_barrier
    after = lax.optimization_barrier
    pieces = cut_page(place, pool_keys, pool_values, chunks)
    units, tokens = [], None
    for c in range(chunks):
        if c:
            pieces[c], units[0] = after((pieces[c], units[0]))
        swapped = swap(pieces[c], "seq")
        if not c:
            swapped[1], turn_table = after((swapped[1], table))
            tokens = rotate_and_cut(
                place, turn_table, freq, queries, keys, values, tp, chunks, prefix
            )
            swapped, tokens = after((swapped, tokens))
        units.append(stacked(swapped))
    gathered = [gather(unit, lines) for unit in units]
    cuts = []
    for c in range(chunks):
        if c:
            tokens[c], tokens[c - 1] = after((tokens[c], tokens[c - 1]))
        tokens[c] = swap(tokens[c], "tp")
        cuts.append(cut_quarters(place, tokens[c]))
    new_keys, new_values = join_outputs(place, tokens, pool_keys.shape[2])
    backs = []
    for c in range(chunks):
        parts = swap(cuts[c], "seq")
        block = parts[0].shape[0] * 2 // 3
        last = last_of(place, parts, block)
        if c + 1 < chunks:
            last, cuts[c + 1] = after((last, cuts[c + 1]))
        if lines == 4:
            early = [along(last, [(0, 1), (2, 3)]), along(last, [(1, 2)])]
        else:
            early = [along(last, [(i, i + 1) for i in range(lines - 1)])]
        if c:
            backs[-1], parts = after((backs[-1], parts))
        outs = attend(place, page_table, table, parts, early, gathered[c], c, lines, page, rows)
        backs.append(cut_back(place, swap(outs, "seq"), tp))
    backs = [swap(back, "tp") for back in backs]
    return join(place, backs, tp, chunks), new_keys, new_values


def solution(mesh):
    return jax.shard_map(
        local,
        mesh=mesh,
        in_specs=(
            P(("seq", "tp"), None),
            P(("seq", "tp"), None),
            P(("seq", "tp"), None),
            P("seq", None, "tp"),
            P("seq", None, "tp"),
            P(),
            P(),
            P(),
        ),
        out_specs=(P(("seq", "tp"), None), P("seq", "tp"), P("seq", "tp")),
        check_vma=False,
    )
```

```python
import functools

import jax
import jax.numpy as jnp
from jax import lax
from jax.experimental import pallas as pl
from jax.experimental.pallas import tpu as pltpu
from jax.sharding import PartitionSpec as P

HD = 96
ROT = 24
SLAB = 4
LOG2E = 1.4426950408889634
VMEM = pl.BlockSpec(memory_space=pltpu.VMEM)
ANY = pl.BlockSpec(memory_space=pl.ANY)
SMEM = pl.BlockSpec(memory_space=pltpu.SMEM)


def params(mib):
    return pltpu.CompilerParams(vmem_limit_bytes=mib << 20)


def shape(rows, lanes):
    return jax.ShapeDtypeStruct((rows, lanes), jnp.bfloat16)


def cost(flops, moved, exps=0):
    return pl.CostEstimate(flops=1, bytes_accessed=1, transcendentals=0)


def starts_and_groups(rows, table):
    starts, ends, groups = table[0:1], table[1:2], table[2:3]
    start = jnp.max(jnp.where(ends <= rows, ends, 0.0), axis=1, keepdims=True)
    inside = (starts <= rows) & (rows < ends)
    group = jnp.sum(jnp.where(inside, groups, 0.0), axis=1, keepdims=True)
    return start, group


def lanes_at(ref, index, each, count, *lead):
    if each % 128 == 0:
        return ref[(*lead, slice(None), pl.ds(pl.multiple_of(index * each, each), each))]
    x = ref[(*lead, slice(None), slice(0, each))]
    for i in range(1, count):
        x = jnp.where(index == i, ref[(*lead, slice(None), slice(i * each, (i + 1) * each))], x)
    return x


def loaded(pairs, sems):
    copies = []
    for i, (source, target) in enumerate(pairs):
        copies.append(pltpu.make_async_copy(source, target, sems.at[i]))
        copies[-1].start()
    return copies


def page_kernel(chunks, place, keys_in, values_in, *refs):
    outs, (keys, values, sems) = refs[:-3], refs[-3:]
    for copy in loaded([(keys_in, keys), (values_in, values)], sems):
        copy.wait()
    lanes = keys.shape[-1] // SLAB
    half = lanes // chunks
    for n in range(SLAB):
        k = lanes_at(keys, place[1] ^ n, lanes, SLAB, 0)
        v = lanes_at(values, place[1] ^ n, lanes, SLAB, 0)
        for c in range(chunks):
            cut = slice(c * half, (c + 1) * half)
            pair = [k[:, cut], v[:, cut]]
            outs[c * SLAB + n][...] = jnp.concatenate(pair[::-1] if c else pair, axis=1)


def cut_page(place, keys, values, chunks):
    lanes = keys.shape[-1] // SLAB // chunks * 2
    outs = pl.pallas_call(
        functools.partial(page_kernel, chunks),
        out_shape=[shape(keys.shape[1], lanes)] * (SLAB * chunks),
        in_specs=[SMEM, ANY, ANY],
        out_specs=[VMEM] * (SLAB * chunks),
        scratch_shapes=[pltpu.VMEM(keys.shape, keys.dtype)] * 2 + [pltpu.SemaphoreType.DMA((2,))],
        compiler_params=params(52),
        cost_estimate=cost(0, 4 * keys.size),
    )(place, keys, values)
    return [outs[c * SLAB : (c + 1) * SLAB] for c in range(chunks)]


def rotate_kernel(tp, chunks, prefix, place, table, freq, queries_in, keys_in, values_in, *refs):
    outs, (queries, keys, values, sems) = refs[:-4], refs[-4:]
    rows, lanes = queries.shape[0], queries.shape[1] // tp
    inputs = ((queries_in, queries), (keys_in, keys), (values_in, values))
    copies = []
    for m in range(tp):
        at = pl.ds(pl.multiple_of((place[3] ^ m) * lanes, lanes), lanes)
        pairs = [(source.at[:, at], target.at[:, at]) for source, target in inputs]
        copies.append(loaded(pairs, sems.at[m]))
    width = freq.shape[1]
    token = place[2] + lax.broadcasted_iota(jnp.int32, (rows, 1), 0)
    token = token.astype(jnp.float32)
    start, _ = starts_and_groups(token, table[...])
    angle = (prefix + token - start) * freq[...]
    dim = lax.rem(lax.broadcasted_iota(jnp.int32, (rows, width), 1), HD)
    cosine, sine = jnp.cos(angle), jnp.sin(angle)
    keep = jnp.where(dim < ROT, cosine, 1.0)
    after = jnp.where(dim < ROT // 2, -sine, 0.0)
    before = jnp.where((dim >= ROT // 2) & (dim < ROT), sine, 0.0)
    cut = width // chunks

    def turned(x):
        x = x.astype(jnp.float32)
        far = pltpu.roll(x, width - ROT // 2, 1)
        near = pltpu.roll(x, ROT // 2, 1)
        return (x * keep + far * after + near * before).astype(jnp.bfloat16)

    for m in range(tp):
        base = (place[3] ^ m) * lanes
        for copy in copies[m]:
            copy.wait()
        for part in range(lanes // width):
            at = pl.ds(pl.multiple_of(base + part * width, width), width)
            q, k, v = turned(queries[:, at]), turned(keys[:, at]), values[:, at]
            quarters = lanes // width == 1 and SLAB or 1
            for i in range(quarters):
                for c in range(chunks):
                    size = cut // quarters
                    of = slice(c * cut + i * size, c * cut + (i + 1) * size)
                    to = slice((part + i) * 2 * size, (part + i + 1) * 2 * size)
                    pair = [k[:, of], v[:, of]]
                    out = outs[c * tp + m]
                    out[:rows, to] = jnp.concatenate(pair[::-1] if c else pair, axis=1)
                    out[rows:, to] = jnp.concatenate([q[: rows // 2, of], q[rows // 2 :, of]], axis=1)


def rotate_and_cut(place, table, freq, queries, keys, values, tp, chunks, prefix):
    rows, lanes = queries.shape[0], queries.shape[1] // tp
    outs = pl.pallas_call(
        functools.partial(rotate_kernel, tp, chunks, prefix),
        out_shape=[shape(rows * 3 // 2, 2 * lanes // chunks)] * (chunks * tp),
        in_specs=[SMEM, VMEM, VMEM, ANY, ANY, ANY],
        out_specs=[VMEM] * (chunks * tp),
        scratch_shapes=[pltpu.VMEM(queries.shape, queries.dtype)] * 3
        + [pltpu.SemaphoreType.DMA((tp, 3))],
        compiler_params=params(52),
        cost_estimate=cost(0, 12 * queries.size),
    )(place, table, freq, queries, keys, values)
    return [outs[c * tp : (c + 1) * tp] for c in range(chunks)]


def quarter_kernel(tp, place, *refs):
    parts, outs = refs[:tp], refs[tp:]
    rows, each = parts[0].shape[0] * 2 // 3, outs[0].shape[1]
    for n in range(SLAB):
        for m in range(tp):
            x = lanes_at(parts[m], place[1] ^ n, each, SLAB)
            to = pl.multiple_of((place[3] ^ m) * rows, rows)
            outs[n][pl.ds(to, rows), :] = x[:rows]
            to = pl.multiple_of(tp * rows + (place[3] ^ m) * (rows // 2), rows // 2)
            outs[n][pl.ds(to, rows // 2), :] = x[rows:]


def cut_quarters(place, parts):
    tp = len(parts)
    rows, lanes = parts[0].shape
    return pl.pallas_call(
        functools.partial(quarter_kernel, tp),
        out_shape=[shape(rows * tp, lanes // SLAB)] * SLAB,
        in_specs=[SMEM] + [VMEM] * tp,
        out_specs=[VMEM] * SLAB,
        compiler_params=params(24),
        cost_estimate=cost(0, 4 * tp * parts[0].size),
    )(place, *parts)


def output_kernel(tp, chunks, place, *refs):
    parts, outs = refs[: chunks * tp], refs[chunks * tp :]
    rows, lanes = outs[0].shape[0] // tp, outs[0].shape[1]
    each = lanes // chunks // SLAB
    for m in range(tp):
        to = pl.ds(pl.multiple_of((place[3] ^ m) * rows, rows), rows)
        for section, out in enumerate(outs):
            pieces = []
            for i in range(SLAB):
                for c in range(chunks):
                    at = 2 * i * each + (each if section != c else 0)
                    pieces.append(parts[c * tp + m][:rows, at : at + each])
            out[to, :] = jnp.concatenate(pieces, axis=1)


def join_outputs(place, parts, lanes):
    chunks, tp = len(parts), len(parts[0])
    rows = parts[0][0].shape[0] * 2 // 3
    return pl.pallas_call(
        functools.partial(output_kernel, tp, chunks),
        out_shape=[shape(rows * tp, lanes)] * 2,
        in_specs=[SMEM] + [VMEM] * (tp * chunks),
        out_specs=[VMEM] * 2,
        compiler_params=params(24),
        cost_estimate=cost(0, 8 * rows * tp * lanes),
    )(place, *[x for chunk in parts for x in chunk])


def stack_kernel(*refs):
    rows = refs[0].shape[0]
    for n, ref in enumerate(refs[:-1]):
        refs[-1][n * rows : (n + 1) * rows, :] = ref[...]


def stacked(parts):
    rows, lanes = parts[0].shape
    return pl.pallas_call(
        stack_kernel,
        out_shape=shape(rows * len(parts), lanes),
        in_specs=[VMEM] * len(parts),
        out_specs=VMEM,
        compiler_params=params(16),
        cost_estimate=cost(0, 4 * len(parts) * parts[0].size),
    )(*parts)


def last_kernel(place, *refs):
    out = refs[-1]
    for n in range(SLAB):

        @pl.when((place[1] ^ n) == SLAB - 1)
        def _():
            out[...] = refs[n][: out.shape[0], :]


def last_of(place, parts, block):
    return pl.pallas_call(
        last_kernel,
        out_shape=shape(block, parts[0].shape[1]),
        in_specs=[SMEM] + [VMEM] * SLAB,
        out_specs=VMEM,
        compiler_params=params(16),
        cost_estimate=cost(0, 4 * block * parts[0].shape[1]),
    )(place, *parts)


def window(lane, count, lanes):
    return lane // 128 * 128, min(-(-(lane + count) // 128) * 128, lanes)


def set_in(x, offset, lanes):
    rows, count = x.shape
    parts = [x]
    if offset:
        parts.insert(0, jnp.zeros((rows, offset), x.dtype))
    if lanes > offset + count:
        parts.append(jnp.zeros((rows, lanes - offset - count), x.dtype))
    return jnp.concatenate(parts, axis=1) if len(parts) > 1 else x


def attend_kernel(plan, place, pages, table, *refs):
    chunk, heads, lines, early_count, unit_count, page, block, rows, served = plan
    parts = refs[:SLAB]
    early = refs[SLAB : SLAB + early_count]
    units = refs[SLAB + early_count : SLAB + early_count + unit_count]
    refs = refs[SLAB + early_count + unit_count :]
    outs, (near_keys, near_values, pool, seat) = refs[:-4], refs[-4:]
    z, j = place[0], place[1]
    slots = lines * SLAB
    middle = (z > 0) & (z < lines - 1)

    half = slots // 2 * page
    width = heads * HD
    key_lane = width if chunk else 0
    value_lane = width - key_lane
    key_low, key_high = window(key_lane, width, 2 * width)
    low, high = window(value_lane, width, 2 * width)
    key_at, value_at = slice(key_low, key_high), slice(low, high)
    factor = HD ** (-0.5) * LOG2E
    contract = (((1,), (1,)), ((), ()))
    first = z * (SLAB * block)

    def dot_t(x, y):
        return lax.dot_general(x, y, contract, preferred_element_type=jnp.float32)

    def dot(x, y):
        return jnp.dot(x, y, preferred_element_type=jnp.float32)

    def fill(i, carry):
        seat[pages[i]] = i
        return carry

    lax.fori_loop(0, slots, fill, 0)

    def set_near(source, at):
        near_keys[pl.ds(at, block), :] = source[:block, key_at]
        near_values[pl.ds(at, block), :] = source[:block, value_at]

    def set_pool(source, line, base):
        for n in range(SLAB):
            to = pl.multiple_of(seat[line * SLAB + (j ^ n)] * page, page)
            pool[pl.ds(to, page), :] = source[base + n * page : base + (n + 1) * page, :]

    for n in range(SLAB):
        set_near(parts[n], pl.multiple_of(((j ^ n) + 1) * block, block))
    if early_count == 2:
        pl.when(z == 2)(lambda: set_near(early[1], 0))
        pl.when(z != 2)(lambda: set_near(early[0], 0))
    else:
        set_near(early[0], 0)
    if unit_count == 6:
        own, a1, b1, a2, b2, a3 = units
        set_pool(own, z, 0)
        set_pool(a1, z ^ 1, 0)
        third, fourth = jnp.where(z < 2, 2, 1), jnp.where(z < 2, 3, 0)

        @pl.when(middle)
        def _():
            set_pool(b1, third, 0)
            set_pool(b2, fourth, 0)

        @pl.when(jnp.logical_not(middle))
        def _():
            set_pool(a2, third, 0)
            set_pool(a3, fourth, 0)
    else:
        for line in range(lines):
            set_pool(units[0], line, line * SLAB * page)

    for out, n in zip(outs, served):
        b = j ^ n
        token = first + b * block + lax.broadcasted_iota(jnp.int32, (block, 1), 0)
        request_start, group = starts_and_groups(token.astype(jnp.float32), table[...])
        zero_group = group < 0.5
        key = first + (b - 1) * block + lax.broadcasted_iota(jnp.int32, (block, 2 * block), 1)
        near = (key >= request_start.astype(jnp.int32)) & (key <= token)
        near_rows = pl.ds(pl.multiple_of(b * block, block), 2 * block)
        folded = parts[n][block:, :]
        halves = []
        for at in range(0, block // 2, rows // 2):
            some = folded[at : at + rows // 2]
            halves += [some[:, :width], some[:, width:]]
        queries = jnp.concatenate(halves, axis=0)
        queries = set_in(queries, key_lane - key_low, key_high - key_low)
        lane = key_low + lax.broadcasted_iota(jnp.int32, queries.shape, 1)
        out_lane = low + lax.broadcasted_iota(jnp.int32, (block, high - low), 1)
        result = jnp.zeros((block, high - low), jnp.float32)
        for h in range(heads):
            begin = key_lane + h * HD
            query = jnp.where((lane >= begin) & (lane < begin + HD), queries, jnp.zeros_like(queries))
            score = jnp.where(
                zero_group,
                dot_t(query, pool[0:half, key_at]),
                dot_t(query, pool[half : 2 * half, key_at]),
            )
            near_score = jnp.where(near, dot_t(query, near_keys[near_rows, :]), -1e30)
            top = jnp.maximum(
                jnp.max(score, axis=1, keepdims=True), jnp.max(near_score, axis=1, keepdims=True)
            )
            weight = jnp.exp2((score - top) * factor)
            near_weight = jnp.exp2((near_score - top) * factor)
            total = jnp.sum(weight, axis=1, keepdims=True) + jnp.sum(
                near_weight, axis=1, keepdims=True
            )
            narrow = weight.astype(jnp.bfloat16)
            nothing = jnp.zeros_like(narrow)
            mixed = (
                dot(jnp.where(zero_group, narrow, nothing), pool[0:half, value_at])
                + dot(jnp.where(zero_group, nothing, narrow), pool[half : 2 * half, value_at])
                + dot(near_weight.astype(jnp.bfloat16), near_values[near_rows, :])
            )
            begin = value_lane + h * HD
            inside = (out_lane >= begin) & (out_lane < begin + HD)
            result = jnp.where(inside, mixed / total, result)
        result = result[:, value_lane - low : value_lane - low + width].astype(jnp.bfloat16)
        folded = jnp.concatenate([result[: block // 2], result[block // 2 :]], axis=1)
        out[...] = folded


def attend(place, pages, table, parts, early, units, chunk, lines, page, rows, served):
    block, width = parts[0].shape[0] * 2 // 3, parts[0].shape[1] // 2
    heads = width // HD
    slots = lines * SLAB
    key_low, key_high = window(width if chunk else 0, width, 2 * width)
    low, high = window(0 if chunk else width, width, 2 * width)
    plan = (chunk, heads, lines, len(early), len(units), page, block, rows, served)
    keys = slots * page + 2 * block
    return pl.pallas_call(
        functools.partial(attend_kernel, plan),
        out_shape=[shape(block // 2, 2 * width)] * len(served),
        in_specs=[SMEM, SMEM, VMEM] + [VMEM] * (SLAB + len(early) + len(units)),
        out_specs=[VMEM] * len(served),
        scratch_shapes=[
            pltpu.VMEM(((SLAB + 1) * block, key_high - key_low), jnp.bfloat16),
            pltpu.VMEM(((SLAB + 1) * block, high - low), jnp.bfloat16),
            pltpu.VMEM((slots * page, 2 * width), jnp.bfloat16),
            pltpu.SMEM((slots,), jnp.int32),
        ],
        compiler_params=params(32),
        cost_estimate=cost(
            4 * SLAB * block * keys * heads * 256,
            4 * keys * width,
            SLAB * block * heads * (keys // 2),
        ),
    )(place, pages, table, *parts, *early, *units)


def back_kernel(tp, place, *refs):
    parts, outs = refs[:SLAB], refs[SLAB:]
    rows, lanes = parts[0].shape
    each = 2 * rows // tp
    for m in range(tp):
        first = (place[3] ^ m) * each
        upper = first >= rows
        at = pl.ds(pl.multiple_of(jnp.where(upper, first - rows, first), each), each)
        cuts = []
        for n in range(SLAB):
            x = parts[n][at, :]
            cuts.append(jnp.where(upper, x[:, lanes // 2 :], x[:, : lanes // 2]))
        outs[m][...] = jnp.concatenate(cuts, axis=1)


def cut_back(place, parts, tp):
    rows, lanes = parts[0].shape
    return pl.pallas_call(
        functools.partial(back_kernel, tp),
        out_shape=[shape(2 * rows // tp, lanes // 2 * SLAB)] * tp,
        in_specs=[SMEM] + [VMEM] * SLAB,
        out_specs=[VMEM] * tp,
        compiler_params=params(16),
        cost_estimate=cost(0, 4 * SLAB * rows * lanes),
    )(place, *parts)


def join_kernel(tp, chunks, place, *refs):
    out = refs[-1]
    lanes = out.shape[1] // tp
    each = lanes // SLAB
    cut = each // chunks
    for m in range(tp):
        for n in range(SLAB):
            base = (place[3] ^ m) * lanes + (place[1] ^ n) * each
            pieces = [refs[c * tp + m][:, n * cut : (n + 1) * cut] for c in range(chunks)]
            x = jnp.concatenate(pieces, axis=1) if chunks > 1 else pieces[0]
            if each % 128:
                for i in range(tp * SLAB):

                    @pl.when(base == i * each)
                    def _():
                        out[:, i * each : (i + 1) * each] = x
            else:
                out[:, pl.ds(pl.multiple_of(base, each), each)] = x


def join(place, parts, tp, chunks):
    rows, lanes = parts[0][0].shape
    return pl.pallas_call(
        functools.partial(join_kernel, tp, chunks),
        out_shape=shape(rows, lanes * tp * chunks),
        in_specs=[SMEM] + [VMEM] * (tp * chunks),
        out_specs=VMEM,
        compiler_params=params(16),
        cost_estimate=cost(0, 4 * rows * lanes * tp * chunks),
    )(place, *[x for chunk in parts for x in chunk])


def swap(parts, axis):
    size = lax.axis_size(axis)
    return [parts[0]] + [
        lax.ppermute(parts[m], axis, [(i, i ^ m) for i in range(size)])
        for m in range(1, len(parts))
    ]


def along(block, pairs):
    return lax.ppermute(
        block, "seq", [(a * SLAB + j, b * SLAB + j) for a, b in pairs for j in range(SLAB)]
    )


INNER = [(1, 2), (2, 1)]
OUTER = [(0, 1), (1, 0), (2, 3), (3, 2)]
OUTWARD = [(1, 0), (2, 3)]


def gather(unit, lines):
    if lines == 4:
        a1 = along(unit, OUTER)
        b1 = along(unit, INNER)
        b2 = along(a1, INNER)
        a2 = along(b1, OUTWARD)
        a3 = along(b2, OUTWARD)
        return [unit, a1, b1, a2, b2, a3]
    groups = [[line * SLAB + j for line in range(lines)] for j in range(SLAB)]
    return [lax.all_gather(unit, "seq", axis=0, axis_index_groups=groups, tiled=True)]


def local(queries, keys, values, pool_keys, pool_values, page_table, lengths, group_of):
    seq, tp = lax.axis_size("seq"), lax.axis_size("tp")
    lines = seq // SLAB
    rows = queries.shape[0]
    page = pool_keys.shape[1]
    own_heads = pool_keys.shape[2] // SLAB // HD
    chunks = 2 if own_heads % 2 == 0 else 1
    index, y = lax.axis_index("seq"), lax.axis_index("tp")
    j = index % SLAB
    place = jnp.stack([index // SLAB, j, (index * tp + y) * rows, y]).astype(jnp.int32)
    ends = jnp.cumsum(lengths)
    table = jnp.stack([ends - lengths, ends, group_of]).astype(jnp.float32)
    width = pool_keys.shape[2] // SLAB
    if width % 128:
        width = pool_keys.shape[2]
    dims = (jnp.arange(width) % HD) % (ROT // 2)
    freq = (10000.0 ** (-(dims.astype(jnp.float32) * 2.0 / ROT)))[None]
    prefix = seq // 2 * page

    after = lax.optimization_barrier
    after = lax.optimization_barrier
    after = lax.optimization_barrier
    pieces = cut_page(place, pool_keys, pool_values, chunks)
    units, tokens = [], None
    for c in range(chunks):
        if c:
            pieces[c], units[0] = after((pieces[c], units[0]))
        swapped = swap(pieces[c], "seq")
        if not c:
            swapped[1], turn_table = after((swapped[1], table))
            tokens = rotate_and_cut(
                place, turn_table, freq, queries, keys, values, tp, chunks, prefix
            )
            swapped, tokens = after((swapped, tokens))
        units.append(stacked(swapped))
    gathered = [gather(unit, lines) for unit in units]
    cuts = []
    for c in range(chunks):
        if c:
            tokens[c], tokens[c - 1] = after((tokens[c], tokens[c - 1]))
        tokens[c] = swap(tokens[c], "tp")
        cuts.append(cut_quarters(place, tokens[c]))
    new_keys, new_values = join_outputs(place, tokens, pool_keys.shape[2])
    backs = []
    for c in range(chunks):
        parts = swap(cuts[c], "seq")
        block = parts[0].shape[0] * 2 // 3
        last = last_of(place, parts, block)
        if c + 1 < chunks:
            last, cuts[c + 1] = after((last, cuts[c + 1]))
        if lines == 4:
            early = [along(last, [(0, 1), (2, 3)]), along(last, [(1, 2)])]
        else:
            early = [along(last, [(i, i + 1) for i in range(lines - 1)])]
        if c:
            backs[-1], parts = after((backs[-1], parts))
        outs = []
        for served in ((2, 3, 1, 0),):
            outs += attend(
                place, page_table, table, parts, early, gathered[c], c, lines, page, rows, served
            )
        outs = outs[::-1]
        outs[2], outs[3] = outs[3], outs[2]
        backs.append(cut_back(place, swap(outs, "seq"), tp))
    backs = [swap(back, "tp") for back in backs]
    return join(place, backs, tp, chunks), new_keys, new_values


def solution(mesh):
    return jax.shard_map(
        local,
        mesh=mesh,
        in_specs=(
            P(("seq", "tp"), None),
            P(("seq", "tp"), None),
            P(("seq", "tp"), None),
            P("seq", None, "tp"),
            P("seq", None, "tp"),
            P(),
            P(),
            P(),
        ),
        out_specs=(P(("seq", "tp"), None), P("seq", "tp"), P("seq", "tp")),
        check_vma=False,
    )
```
